256 devices in a mesh: layer: 4 (over y_lo, core), train: 8 (over y_hi, x), query: 8 (over z).
Axes of the slice: x: 4, y: 4 (y_hi: 2, y_lo: 2; y = y_hi * 2 + y_lo), z: 8, core: 2. Of those that a mesh axis runs over, the one named last changes fastest.
Arguments:
- train_act: bfloat16 [2, 4, 64, 128, 4096], P(None, 'layer', ('train', 'query')), may hold values from -6 to 6
- train_grad: bfloat16 [2, 4, 64, 128, 4096], P(None, 'layer', ('train', 'query')), may hold values from -6 to 6
- query_act: bfloat16 [2, 4, 64, 128, 4096], P(None, 'layer', ('train', 'query')), may hold values from -6 to 6
- query_grad: bfloat16 [2, 4, 64, 128, 4096], P(None, 'layer', ('train', 'query')), may hold values from -6 to 6
- in_projection: bfloat16 [4, 4096, 128], P('layer'), may hold values from -0.09375 to 0.09375
- out_projection: bfloat16 [4, 4096, 64], P('layer'), may hold values from -0.09375 to 0.09375
- inverse_hessian: bfloat16 [2, 8192, 8192], P(None, 'layer', ('train', 'query'))
- train_lengths: int32 [64], P(('train', 'query')), may hold values from 16 to 128
- query_lengths: int32 [64], P(('train', 'query')), may hold values from 16 to 128
Outputs:
- scores: float32 [64, 64], P('train', 'query')
The draws below stay inside these ranges and needn't reach their ends.
All inputs are finite; a program needn't handle non-finite values.
Results may differ from the reference program's by a relative error of at most 0.0071.
Values may be sent and summed in bfloat16 or wider, within the bound.
No kernel may reach another device: no remote copies, remote signals or barrier semaphores. Data moves between devices by JAX's collectives and lax.ppermute only.
A program may use at most 64 MiB of HBM per device.

```python
import jax
import jax.numpy as jnp
from jax import lax

D = 4096
KIN = 128
KOUT = 64
FEAT = 8192
SEQ = 128
CKPT = 2
LAYERS = 4
NTR = 64
NQ = 64


def draw_inverse_hessian(key, part):
    key = jax.random.fold_in(key, 7)
    noise_key, diagonal_key = jax.random.split(key)
    noise = jax.random.normal(noise_key, (CKPT, FEAT, FEAT), jnp.float32)
    noise = 0.5 * (noise + jnp.swapaxes(noise, 1, 2)) * (0.8 / jnp.sqrt(jnp.float32(FEAT)))
    diagonal = jnp.exp(jax.random.uniform(diagonal_key, (CKPT, FEAT), jnp.float32, jnp.log(0.5), jnp.log(2.0)))
    rows = lax.broadcasted_iota(jnp.int32, (FEAT, FEAT), 0)
    columns = lax.broadcasted_iota(jnp.int32, (FEAT, FEAT), 1)
    return (jnp.where((rows == columns)[None, :, :], diagonal[:, :, None], 0.0) + noise).astype(jnp.bfloat16)


def plant(values, rng, smallest, high):
    longest = values.shape.index(max(values.shape))
    spots = []
    for shift in (0, 1):
        where = [jax.random.randint(jax.random.fold_in(rng, axis), (), 0, length) for axis, length in enumerate(values.shape)]
        where[longest] = (where[longest] + shift) % values.shape[longest]
        spots.append(tuple(where))
    return values.at[spots[0]].set(smallest).at[spots[1]].set(high)


def level_of(rng, extent, shards, low, top_value):
    def one(axis_at, parts):
        draws = jax.random.uniform(jax.random.fold_in(jax.random.fold_in(rng, 6), axis_at), (parts,), jnp.float32, low / len(shards), top_value / len(shards))
        return jnp.repeat(jnp.exp(draws), extent[axis_at] // parts).reshape((-1,) + (1,) * (len(extent) - axis_at - 1))

    gain = one(*shards[0])
    for cut in shards[1:]:
        gain = gain * one(*cut)
    return gain


def bell_draw(key, dims, width, most, pieces=(), held_as=jnp.bfloat16):
    result = jax.random.normal(key, dims, jnp.float32) * width
    if len(pieces) > 0:
        result = level_of(key, dims, pieces, -0.22, 0.18) * result
    return jnp.clip(result, min=-most, max=most).astype(held_as)


def setup_inputs(seed: int = 0) -> dict:
    splits = jax.random.split(jax.random.key(seed), 10)
    return {
        "train_act": bell_draw(splits[0], (CKPT, LAYERS, NTR, SEQ, D), 1.0, 6.0, ((1, 4), (2, 64))),
        "train_grad": bell_draw(splits[1], (CKPT, LAYERS, NTR, SEQ, D), 1.0, 6.0, ((1, 4), (2, 64))),
        "query_act": bell_draw(splits[2], (CKPT, LAYERS, NQ, SEQ, D), 1.0, 6.0, ((1, 4), (2, 64))),
        "query_grad": bell_draw(splits[3], (CKPT, LAYERS, NQ, SEQ, D), 1.0, 6.0, ((1, 4), (2, 64))),
        "in_projection": bell_draw(splits[4], (LAYERS, D, KIN), D ** -0.5, 0.09375, ((0, 4),)),
        "out_projection": bell_draw(splits[5], (LAYERS, D, KOUT), D ** -0.5, 0.09375, ((0, 4),)),
        "inverse_hessian": draw_inverse_hessian(jax.random.fold_in(splits[9], 71), 0),
        "train_lengths": plant(jax.random.randint(splits[7], (NTR,), max(1, SEQ // 8), SEQ + 1), jax.random.fold_in(splits[7], 1), max(1, SEQ // 8), SEQ).astype(jnp.int32),
        "query_lengths": plant(jax.random.randint(splits[8], (NQ,), max(1, SEQ // 8), SEQ + 1), jax.random.fold_in(splits[8], 1), max(1, SEQ // 8), SEQ).astype(jnp.int32),
    }


def features(activations, gradients, in_projection, out_projection, lengths):
    count = activations.shape[1]
    positions = jnp.arange(SEQ, dtype=jnp.int32)
    keep_mask = positions[None, :] < lengths[:, None]
    total = jnp.zeros((count, KOUT, KIN), jnp.float32)
    for layer_slot in range(LAYERS):
        inner = jnp.dot(activations[layer_slot].reshape(count * SEQ, D), in_projection[layer_slot], preferred_element_type=jnp.float32).astype(jnp.bfloat16)
        outer = jnp.dot(gradients[layer_slot].reshape(count * SEQ, D), out_projection[layer_slot], preferred_element_type=jnp.float32)
        outer = jnp.where(keep_mask[:, :, None], outer.reshape(count, SEQ, KOUT), 0.0).astype(jnp.bfloat16)
        total = total + jnp.einsum('nso,nsi->noi', outer.astype(jnp.float32), inner.reshape(count, SEQ, KIN).astype(jnp.float32))
    return (total.reshape(count, FEAT) / SEQ).astype(jnp.bfloat16)


def reference(train_act, train_grad, query_act, query_grad, in_projection, out_projection, inverse_hessian, train_lengths, query_lengths):
    scores = jnp.zeros((NTR, NQ), jnp.float32)
    for checkpoint in range(CKPT):
        train_features = features(train_act[checkpoint], train_grad[checkpoint], in_projection, out_projection, train_lengths)
        query_features = features(query_act[checkpoint], query_grad[checkpoint], in_projection, out_projection, query_lengths)
        preconditioned = jnp.dot(train_features, inverse_hessian[checkpoint], preferred_element_type=jnp.float32)
        scores = scores + jnp.dot(preconditioned, query_features.astype(jnp.float32).T, precision=lax.Precision.HIGHEST, preferred_element_type=jnp.float32)
    return scores
```

```python
import jax
import jax.numpy as jnp
from jax import lax
from jax.sharding import PartitionSpec as P


def sketch(activations, gradients, in_projection, out_projection, lengths):
    ckpt_count, _, row_count, seq_len, width = activations.shape
    positions = lax.broadcasted_iota(jnp.int32, (row_count, seq_len), 1)
    keep_mask = (positions < lengths[:, None]).reshape(1, row_count * seq_len, 1)
    flat_act = activations.reshape(ckpt_count, row_count * seq_len, width)
    flat_grad = gradients.reshape(ckpt_count, row_count * seq_len, width)
    inner = jnp.einsum(
        "cnd,dk->cnk", flat_act, in_projection[0], preferred_element_type=jnp.float32
    ).astype(jnp.bfloat16)
    outer = jnp.einsum(
        "cnd,dk->cnk", flat_grad, out_projection[0], preferred_element_type=jnp.float32
    )
    outer = jnp.where(keep_mask, outer, 0.0).astype(jnp.bfloat16)
    return jnp.einsum("cso,csi->coi", outer, inner, preferred_element_type=jnp.float32)


def on_device(
    train_act,
    train_grad,
    query_act,
    query_grad,
    in_projection,
    out_projection,
    inverse_hessian,
    train_lengths,
    query_lengths,
):
    seq_len = train_act.shape[3]
    layers = lax.axis_size("layer")
    rows_a, cols_b = lax.axis_size("train"), lax.axis_size("query")
    grid = rows_a * cols_b
    train_terms = sketch(train_act, train_grad, in_projection, out_projection, train_lengths)
    query_terms = sketch(query_act, query_grad, in_projection, out_projection, query_lengths)
    both = lax.all_gather(jnp.stack([train_terms, query_terms]), "layer")
    features = (jnp.sum(both, axis=0) / seq_len).astype(jnp.bfloat16)
    ckpts, outs, ins = train_terms.shape
    block = outs // layers
    layer_index = lax.axis_index("layer")
    train_block = lax.dynamic_slice_in_dim(features[0], layer_index * block, block, 1)
    train_message = jnp.broadcast_to(train_block[None], (grid, ckpts, block, ins))
    query_message = jnp.transpose(features[1], (1, 0, 2))[:, :, None, :]
    message = jnp.concatenate([train_message, query_message], axis=2)
    received = lax.all_to_all(message, ("train", "query"), 0, 0)
    train_rows = received[:, :, :block]
    query_columns = received[:, :, block]
    hessian = inverse_hessian.reshape(ckpts, block, ins, -1)
    partial_pre = jnp.einsum(
        "tcki,ckin->ctn", train_rows, hessian, preferred_element_type=jnp.float32
    )
    terms = jnp.einsum(
        "ctn,qcn->tq",
        partial_pre,
        query_columns.astype(jnp.float32),
        precision=lax.Precision.HIGHEST,
        preferred_element_type=jnp.float32,
    )
    tile_rows = terms.shape[0] // rows_a
    tile_cols = terms.shape[1] // cols_b
    tiles = terms.reshape(rows_a, tile_rows, cols_b, tile_cols)
    tiles = jnp.transpose(tiles, (0, 2, 1, 3)).reshape(1, grid, 1, tile_rows * tile_cols)
    tiles = jnp.broadcast_to(tiles, (layers, grid, 1, tile_rows * tile_cols))
    tiles = tiles.reshape(layers * grid, 1, tile_rows * tile_cols)
    shares = lax.all_to_all(tiles, ("layer", "train", "query"), 0, 0)
    return jnp.sum(shares, axis=0).reshape(tile_rows, tile_cols)


def solution(mesh):
    tokens = P(None, "layer", ("train", "query"), None, None)
    in_specs = (
        tokens,
        tokens,
        tokens,
        tokens,
        P("layer", None, None),
        P("layer", None, None),
        P(None, "layer", ("train", "query")),
        P(("train", "query")),
        P(("train", "query")),
    )
    return jax.shard_map(
        on_device, mesh=mesh, in_specs=in_specs, out_specs=P("train", "query"), check_vma=False
    )
```

```python
import jax
import jax.numpy as jnp
from jax import lax
from jax.experimental import pallas as pl
from jax.experimental.pallas import tpu as pltpu
from jax.sharding import PartitionSpec as P

CHUNKS = 4
AHEAD = 3


def sketch_kernel(
    train_length,
    query_length,
    train_act,
    train_grad,
    query_act,
    query_grad,
    in_projection,
    out_projection,
    result,
    act,
    grad,
    in_weights,
    out_weights,
    inner,
    outer,
    arrived,
):
    ckpts, seq_len, width = train_act.shape
    chunk = width // CHUNKS
    rows = 2 * ckpts * seq_len
    copies = []
    for step in range(CHUNKS):
        cols = pl.ds(step * chunk, chunk)
        group = [
            (in_projection.at[cols], in_weights.at[cols]),
            (train_act.at[:, :, cols], act.at[pl.ds(0, ckpts), :, cols]),
            (query_act.at[:, :, cols], act.at[pl.ds(ckpts, ckpts), :, cols]),
            (out_projection.at[:, cols], out_weights.at[:, cols]),
            (train_grad.at[:, :, cols], grad.at[pl.ds(0, ckpts), :, cols]),
            (query_grad.at[:, :, cols], grad.at[pl.ds(ckpts, ckpts), :, cols]),
        ]
        group = [
            pltpu.make_async_copy(source, target, arrived.at[step, place])
            for place, (source, target) in enumerate(group)
        ]
        copies.append(group)
    for group in copies[:AHEAD]:
        for copy in group:
            copy.start()
    for step, group in enumerate(copies):
        cols = pl.ds(step * chunk, chunk)
        for copy in group:
            copy.wait()
        for ahead in copies[step + AHEAD : step + AHEAD + 1]:
            for copy in ahead:
                copy.start()
        inner_term = jnp.dot(
            act[:, :, cols].reshape(rows, chunk),
            in_weights[cols],
            preferred_element_type=jnp.float32,
        )
        outer_term = lax.dot_general(
            grad[:, :, cols].reshape(rows, chunk),
            out_weights[:, cols],
            (((1,), (1,)), ((), ())),
            preferred_element_type=jnp.float32,
        )
        if step == 0:
            inner[...] = inner_term
            outer[...] = outer_term
        else:
            inner[...] += inner_term
            outer[...] += outer_term
    for side, length in enumerate((train_length, query_length)):
        for ckpt in range(ckpts):
            part = pl.ds((side * ckpts + ckpt) * seq_len, seq_len)
            kept = outer[part]
            positions = lax.broadcasted_iota(jnp.int32, kept.shape, 0)
            kept = jnp.where(positions < length[0], kept, 0.0).astype(jnp.bfloat16)
            total = lax.dot_general(
                kept,
                inner[part].astype(jnp.bfloat16),
                (((0,), (0,)), ((), ())),
                preferred_element_type=jnp.float32,
            )
            result[side, ckpt] = total.astype(result.dtype)


def sketches(train_act, train_grad, query_act, query_grad, in_projection, out_projection, train_length, query_length):
    ckpts, _, _, seq_len, width = train_act.shape
    ins, outs = in_projection.shape[2], out_projection.shape[2]
    flat = [x.reshape(ckpts, seq_len, width) for x in (train_act, train_grad, query_act, query_grad)]
    stay = pl.BlockSpec(memory_space=pl.ANY)
    scalar = pl.BlockSpec(memory_space=pltpu.SMEM)
    rows = 2 * ckpts * seq_len
    return pl.pallas_call(
        sketch_kernel,
        out_shape=jax.ShapeDtypeStruct((2, ckpts, outs, ins), jnp.bfloat16),
        in_specs=[scalar, scalar] + [stay] * 6,
        out_specs=pl.BlockSpec(memory_space=pltpu.VMEM),
        scratch_shapes=[
            pltpu.VMEM((2 * ckpts, seq_len, width), jnp.bfloat16),
            pltpu.VMEM((2 * ckpts, seq_len, width), jnp.bfloat16),
            pltpu.VMEM((width, ins), jnp.bfloat16),
            pltpu.VMEM((outs, width), jnp.bfloat16),
            pltpu.VMEM((rows, ins), jnp.float32),
            pltpu.VMEM((rows, outs), jnp.float32),
            pltpu.SemaphoreType.DMA((CHUNKS, 6)),
        ],
        compiler_params=pltpu.CompilerParams(vmem_limit_bytes=60 * 1024 * 1024),
        name="sketches",
    )(train_length, query_length, *flat, in_projection[0], out_projection[0].T)


def on_device(
    train_act,
    train_grad,
    query_act,
    query_grad,
    in_projection,
    out_projection,
    inverse_hessian,
    train_lengths,
    query_lengths,
):
    seq_len = train_act.shape[3]
    layers = lax.axis_size("layer")
    rows_a, cols_b = lax.axis_size("train"), lax.axis_size("query")
    grid = rows_a * cols_b
    terms = sketches(
        train_act, train_grad, query_act, query_grad, in_projection, out_projection, train_lengths, query_lengths
    )
    _, ckpts, outs, ins = terms.shape
    block = outs // layers
    half = block // 2
    pairs = cols_b // 2
    parity = lax.rem(lax.axis_index("query"), 2)
    hessian = inverse_hessian.reshape(ckpts, 2, half, ins, -1)
    other_half = lax.dynamic_index_in_dim(hessian, 1 - parity, 1, keepdims=False)
    swap = [(i, i ^ 1) for i in range(cols_b)]
    hessian_other = lax.ppermute(other_half, "query", swap)
    hessian_own = lax.dynamic_index_in_dim(hessian, parity, 1, keepdims=False)
    layer_index = lax.axis_index("layer")
    gathered = lax.all_gather(terms, "layer")
    total = jnp.sum(gathered.astype(jnp.float32), axis=0) / seq_len
    features = jnp.concatenate(
        [lax.dynamic_slice_in_dim(total[0], layer_index * block, block, 1), total[1]], axis=1
    ).astype(jnp.bfloat16)
    train_block = jnp.transpose(features[:, :block].reshape(ckpts, 2, half, ins), (1, 2, 0, 3))
    train_message = jnp.broadcast_to(train_block[None, :, None], (pairs, 2, rows_a, half, ckpts, ins))
    train_message = train_message.reshape(grid, half, ckpts, ins)
    query = features[:, block:].reshape(ckpts, rows_a, pairs, 2, ins)
    query_own = jnp.transpose(query, (2, 3, 1, 0, 4)).reshape(grid, 1, ckpts, ins)
    query_other = jnp.transpose(jnp.flip(query, 3), (2, 3, 1, 0, 4)).reshape(grid, 1, ckpts, ins)
    message = jnp.concatenate([train_message, query_own, query_other], axis=1)
    message, hessian_other = lax.optimization_barrier((message, hessian_other))
    received = lax.all_to_all(message, ("query", "train"), 0, 0)
    train_rows = received[:, :half]
    query_columns = jnp.concatenate([received[:, half], received[:, half + 1]], axis=2)
    partial_pre = jnp.concatenate(
        [
            jnp.einsum("tkci,ckin->ctn", train_rows, part, preferred_element_type=jnp.float32)
            for part in (hessian_own, hessian_other)
        ],
        axis=2,
    )
    scores = jnp.einsum(
        "ctn,qcn->tq",
        partial_pre,
        query_columns.astype(jnp.float32),
        precision=lax.Precision.HIGHEST,
        preferred_element_type=jnp.float32,
    )
    tile_rows = scores.shape[0] // rows_a
    tile_cols = scores.shape[1] // cols_b
    tiles = scores.reshape(cols_b, rows_a, tile_cols, cols_b)
    tiles = jnp.transpose(tiles, (1, 3, 0, 2)).reshape(1, grid, 1, tile_rows * tile_cols)
    tiles = jnp.broadcast_to(tiles, (layers, grid, 1, tile_rows * tile_cols))
    tiles = tiles.reshape(layers * grid, 1, tile_rows * tile_cols)
    shares = lax.all_to_all(tiles, ("layer", "train", "query"), 0, 0)
    return jnp.sum(shares, axis=0).reshape(tile_rows, tile_cols)


def solution(mesh):
    tokens = P(None, "layer", ("train", "query"), None, None)
    in_specs = (
        tokens,
        tokens,
        tokens,
        tokens,
        P("layer", None, None),
        P("layer", None, None),
        P(None, "layer", ("train", "query")),
        P(("train", "query")),
        P(("train", "query")),
    )
    return jax.shard_map(
        on_device, mesh=mesh, in_specs=in_specs, out_specs=P("train", "query"), check_vma=False
    )
```

```python
import jax
import jax.numpy as jnp
from jax import lax
from jax.experimental import pallas as pl
from jax.experimental.pallas import tpu as pltpu
from jax.sharding import PartitionSpec as P

CHUNKS = 4
AHEAD = 3


def sketch_kernel(
    train_length,
    query_length,
    train_act,
    train_grad,
    query_act,
    query_grad,
    in_projection,
    out_projection,
    result,
    act,
    grad,
    in_weights,
    out_weights,
    inner,
    outer,
    arrived,
):
    ckpts, seq_len, width = train_act.shape
    chunk = width // CHUNKS
    rows = 2 * ckpts * seq_len
    copies = []
    for step in range(CHUNKS):
        cols = pl.ds(step * chunk, chunk)
        group = [
            (in_projection.at[cols], in_weights.at[cols]),
            (train_act.at[:, :, cols], act.at[pl.ds(0, ckpts), :, cols]),
            (query_act.at[:, :, cols], act.at[pl.ds(ckpts, ckpts), :, cols]),
            (out_projection.at[:, cols], out_weights.at[:, cols]),
            (train_grad.at[:, :, cols], grad.at[pl.ds(0, ckpts), :, cols]),
            (query_grad.at[:, :, cols], grad.at[pl.ds(ckpts, ckpts), :, cols]),
        ]
        group = [
            pltpu.make_async_copy(source, target, arrived.at[step, place])
            for place, (source, target) in enumerate(group)
        ]
        copies.append(group)
    for group in copies[:AHEAD]:
        for copy in group:
            copy.start()
    for step, group in enumerate(copies):
        cols = pl.ds(step * chunk, chunk)
        for copy in group:
            copy.wait()
        for ahead in copies[step + AHEAD : step + AHEAD + 1]:
            for copy in ahead:
                copy.start()
        inner_term = jnp.dot(
            act[:, :, cols].reshape(rows, chunk),
            in_weights[cols],
            preferred_element_type=jnp.float32,
        )
        outer_term = lax.dot_general(
            grad[:, :, cols].reshape(rows, chunk),
            out_weights[:, cols],
            (((1,), (1,)), ((), ())),
            preferred_element_type=jnp.float32,
        )
        if step == 0:
            inner[...] = inner_term
            outer[...] = outer_term
        else:
            inner[...] += inner_term
            outer[...] += outer_term
    for side, length in enumerate((train_length, query_length)):
        for ckpt in range(ckpts):
            part = pl.ds((side * ckpts + ckpt) * seq_len, seq_len)
            kept = outer[part]
            positions = lax.broadcasted_iota(jnp.int32, kept.shape, 0)
            kept = jnp.where(positions < length[0], kept, 0.0).astype(jnp.bfloat16)
            total = lax.dot_general(
                kept,
                inner[part].astype(jnp.bfloat16),
                (((0,), (0,)), ((), ())),
                preferred_element_type=jnp.float32,
            )
            result[side, ckpt] = total


def sketches(train_act, train_grad, query_act, query_grad, in_projection, out_projection, train_length, query_length):
    ckpts, _, _, seq_len, width = train_act.shape
    ins, outs = in_projection.shape[2], out_projection.shape[2]
    flat = [x.reshape(ckpts, seq_len, width) for x in (train_act, train_grad, query_act, query_grad)]
    stay = pl.BlockSpec(memory_space=pl.ANY)
    scalar = pl.BlockSpec(memory_space=pltpu.SMEM)
    rows = 2 * ckpts * seq_len
    return pl.pallas_call(
        sketch_kernel,
        out_shape=jax.ShapeDtypeStruct((2, ckpts, outs, ins), jnp.float32),
        in_specs=[scalar, scalar] + [stay] * 6,
        out_specs=pl.BlockSpec(memory_space=pltpu.VMEM),
        scratch_shapes=[
            pltpu.VMEM((2 * ckpts, seq_len, width), jnp.bfloat16),
            pltpu.VMEM((2 * ckpts, seq_len, width), jnp.bfloat16),
            pltpu.VMEM((width, ins), jnp.bfloat16),
            pltpu.VMEM((outs, width), jnp.bfloat16),
            pltpu.VMEM((rows, ins), jnp.float32),
            pltpu.VMEM((rows, outs), jnp.float32),
            pltpu.SemaphoreType.DMA((CHUNKS, 6)),
        ],
        compiler_params=pltpu.CompilerParams(vmem_limit_bytes=60 * 1024 * 1024),
        name="sketches",
    )(train_length, query_length, *flat, in_projection[0], out_projection[0].T)


def add_shares(shares, tile):
    total = jnp.sum(shares[...], axis=0, keepdims=True)
    width = tile.shape[1]
    for row in range(tile.shape[0]):
        tile[pl.ds(row, 1)] = total[:, row * width : (row + 1) * width]


def on_device(
    train_act,
    train_grad,
    query_act,
    query_grad,
    in_projection,
    out_projection,
    inverse_hessian,
    train_lengths,
    query_lengths,
):
    seq_len = train_act.shape[3]
    layers = lax.axis_size("layer")
    rows_a, cols_b = lax.axis_size("train"), lax.axis_size("query")
    grid = rows_a * cols_b
    terms = sketches(
        train_act, train_grad, query_act, query_grad, in_projection, out_projection, train_lengths, query_lengths
    )
    _, ckpts, outs, ins = terms.shape
    block = outs // layers
    half = block // 2
    pairs = rows_a // 2
    parity = lax.rem(lax.axis_index("train"), 2)
    hessian = inverse_hessian.reshape(ckpts, 2, half, ins, -1)
    other_half = lax.dynamic_index_in_dim(hessian, 1 - parity, 1, keepdims=False)
    swap = [(i, i ^ 1) for i in range(rows_a)]
    hessian_other = lax.ppermute(other_half, "train", swap)
    hessian_own = lax.dynamic_index_in_dim(hessian, parity, 1, keepdims=False)
    layer_index = lax.axis_index("layer")
    gathered = lax.all_gather(terms, "layer", axis_index_groups=[[i, i + 1] for i in range(0, layers, 2)])
    terms = gathered[0] + gathered[1]
    outgoing = jnp.concatenate(
        [lax.dynamic_slice_in_dim(terms[0], (layer_index ^ 2) * block, block, 1), terms[1]], axis=1
    ).astype(jnp.bfloat16)
    own = jnp.concatenate(
        [lax.dynamic_slice_in_dim(terms[0], layer_index * block, block, 1), terms[1]], axis=1
    )
    incoming = lax.ppermute(outgoing, "layer", [(i, i ^ 2) for i in range(layers)])
    features = ((own + incoming.astype(jnp.float32)) / seq_len).astype(jnp.bfloat16)
    train_block = jnp.transpose(features[:, :block].reshape(ckpts, 2, half, ins), (1, 2, 0, 3))
    train_message = jnp.broadcast_to(train_block, (cols_b, pairs, 2, half, ckpts, ins))
    train_message = train_message.reshape(grid, half, ckpts, ins)
    query = features[:, block:].reshape(ckpts, pairs, 2, cols_b, ins)
    query_own = jnp.transpose(query, (3, 1, 2, 0, 4)).reshape(grid, 1, ckpts, ins)
    query_other = jnp.transpose(jnp.flip(query, 2), (3, 1, 2, 0, 4)).reshape(grid, 1, ckpts, ins)
    message = jnp.concatenate([train_message, query_own, query_other], axis=1)
    message, hessian_other = lax.optimization_barrier((message, hessian_other))
    received = lax.all_to_all(message, ("query", "train"), 0, 0)
    train_rows = received[:, :half]
    query_columns = jnp.concatenate([received[:, half], received[:, half + 1]], axis=2)
    partial_pre = jnp.concatenate(
        [
            jnp.einsum("tkci,ckin->ctn", train_rows, part, preferred_element_type=jnp.float32)
            for part in (hessian_own, hessian_other)
        ],
        axis=2,
    )
    scores = jnp.einsum(
        "ctn,qcn->tq",
        partial_pre,
        query_columns.astype(jnp.float32),
        precision=lax.Precision.HIGHEST,
        preferred_element_type=jnp.float32,
    )
    tile_rows = scores.shape[0] // rows_a
    tile_cols = scores.shape[1] // cols_b
    tiles = scores.reshape(cols_b, rows_a, tile_cols, cols_b)
    tiles = jnp.transpose(tiles, (1, 3, 0, 2)).reshape(1, grid, 1, tile_rows * tile_cols)
    tiles = jnp.broadcast_to(tiles, (layers, grid, 1, tile_rows * tile_cols))
    tiles = tiles.reshape(layers * grid, 1, tile_rows * tile_cols)
    shares = lax.all_to_all(tiles, ("layer", "train", "query"), 0, 0)
    return pl.pallas_call(
        add_shares,
        out_shape=jax.ShapeDtypeStruct((tile_rows, tile_cols), jnp.float32),
        compiler_params=pltpu.CompilerParams(vmem_limit_bytes=4 * 1024 * 1024),
        name="add_shares",
    )(shares.reshape(layers * grid, tile_rows * tile_cols))


def solution(mesh):
    tokens = P(None, "layer", ("train", "query"), None, None)
    in_specs = (
        tokens,
        tokens,
        tokens,
        tokens,
        P("layer", None, None),
        P("layer", None, None),
        P(None, "layer", ("train", "query")),
        P(("train", "query")),
        P(("train", "query")),
    )
    return jax.shard_map(
        on_device, mesh=mesh, in_specs=in_specs, out_specs=P("train", "query"), check_vma=False
    )
```

```python
import jax
import jax.numpy as jnp
from jax import lax
from jax.experimental import pallas as pl
from jax.experimental.pallas import tpu as pltpu
from jax.sharding import PartitionSpec as P

CHUNKS = 4
AHEAD = 3


def sketch_kernel(
    train_length,
    query_length,
    train_act,
    train_grad,
    query_act,
    query_grad,
    in_projection,
    out_projection,
    result,
    act,
    grad,
    inner,
    outer,
    arrived,
):
    ckpts, seq_len, width = train_act.shape
    chunk = width // CHUNKS
    rows = 2 * ckpts * seq_len
    copies = []
    for step in range(CHUNKS):
        cols = pl.ds(step * chunk, chunk)
        group = [
            (train_act.at[:, :, cols], act.at[pl.ds(0, ckpts), :, cols]),
            (query_act.at[:, :, cols], act.at[pl.ds(ckpts, ckpts), :, cols]),
            (train_grad.at[:, :, cols], grad.at[pl.ds(0, ckpts), :, cols]),
            (query_grad.at[:, :, cols], grad.at[pl.ds(ckpts, ckpts), :, cols]),
        ]
        group = [
            pltpu.make_async_copy(source, target, arrived.at[step, place])
            for place, (source, target) in enumerate(group)
        ]
        copies.append(group)
    for group in copies[:AHEAD]:
        for copy in group:
            copy.start()
    for step, group in enumerate(copies):
        cols = pl.ds(step * chunk, chunk)
        for copy in group:
            copy.wait()
        for ahead in copies[step + AHEAD : step + AHEAD + 1]:
            for copy in ahead:
                copy.start()
        inner_term = jnp.dot(
            act[:, :, cols].reshape(rows, chunk),
            in_projection[cols],
            preferred_element_type=jnp.float32,
        )
        outer_term = lax.dot_general(
            grad[:, :, cols].reshape(rows, chunk),
            out_projection[:, cols],
            (((1,), (1,)), ((), ())),
            preferred_element_type=jnp.float32,
        )
        if step == 0:
            inner[...] = inner_term
            outer[...] = outer_term
        else:
            inner[...] += inner_term
            outer[...] += outer_term
    for side, length in enumerate((train_length, query_length)):
        for ckpt in range(ckpts):
            part = pl.ds((side * ckpts + ckpt) * seq_len, seq_len)
            kept = outer[part]
            positions = lax.broadcasted_iota(jnp.int32, kept.shape, 0)
            kept = jnp.where(positions < length[0], kept, 0.0).astype(jnp.bfloat16)
            total = lax.dot_general(
                kept,
                inner[part].astype(jnp.bfloat16),
                (((0,), (0,)), ((), ())),
                preferred_element_type=jnp.float32,
            )
            result[side, ckpt] = total


def sketches(train_act, train_grad, query_act, query_grad, in_projection, out_projection, train_length, query_length):
    ckpts, _, _, seq_len, width = train_act.shape
    ins, outs = in_projection.shape[2], out_projection.shape[2]
    flat = [x.reshape(ckpts, seq_len, width) for x in (train_act, train_grad, query_act, query_grad)]
    stay = pl.BlockSpec(memory_space=pl.ANY)
    scalar = pl.BlockSpec(memory_space=pltpu.SMEM)
    held = pl.BlockSpec(memory_space=pltpu.VMEM)
    rows = 2 * ckpts * seq_len
    return pl.pallas_call(
        sketch_kernel,
        out_shape=jax.ShapeDtypeStruct((2, ckpts, outs, ins), jnp.float32),
        in_specs=[scalar, scalar] + [stay] * 4 + [held] * 2,
        out_specs=pl.BlockSpec(memory_space=pltpu.VMEM),
        scratch_shapes=[
            pltpu.VMEM((2 * ckpts, seq_len, width), jnp.bfloat16),
            pltpu.VMEM((2 * ckpts, seq_len, width), jnp.bfloat16),
            pltpu.VMEM((rows, ins), jnp.float32),
            pltpu.VMEM((rows, outs), jnp.float32),
            pltpu.SemaphoreType.DMA((CHUNKS, 4)),
        ],
        compiler_params=pltpu.CompilerParams(vmem_limit_bytes=52 * 1024 * 1024),
        name="sketches",
    )(train_length, query_length, *flat, in_projection[0], out_projection[0].T)


def add_shares(shares, tile):
    total = jnp.sum(shares[...], axis=0, keepdims=True)
    width = tile.shape[1]
    for row in range(tile.shape[0]):
        tile[pl.ds(row, 1)] = total[:, row * width : (row + 1) * width]


def on_device(
    train_act,
    train_grad,
    query_act,
    query_grad,
    in_projection,
    out_projection,
    inverse_hessian,
    train_lengths,
    query_lengths,
):
    seq_len = train_act.shape[3]
    layers = lax.axis_size("layer")
    rows_a, cols_b = lax.axis_size("train"), lax.axis_size("query")
    grid = rows_a * cols_b
    terms = sketches(
        train_act, train_grad, query_act, query_grad, in_projection, out_projection, train_lengths, query_lengths
    )
    _, ckpts, outs, ins = terms.shape
    block = outs // layers
    half = block // 2
    pairs = rows_a // 2
    parity = lax.rem(lax.axis_index("train"), 2)
    hessian = inverse_hessian.reshape(ckpts, 2, half, ins, -1)
    other_half = lax.dynamic_index_in_dim(hessian, 1 - parity, 1, keepdims=False)
    swap = [(i, i ^ 1) for i in range(rows_a)]
    hessian_other = lax.ppermute(other_half, "train", swap)
    hessian_own = lax.dynamic_index_in_dim(hessian, parity, 1, keepdims=False)
    layer_index = lax.axis_index("layer")
    gathered = lax.all_gather(terms, "layer", axis_index_groups=[[i, i + 1] for i in range(0, layers, 2)])
    terms = gathered[0] + gathered[1]
    outgoing = jnp.concatenate(
        [lax.dynamic_slice_in_dim(terms[0], (layer_index ^ 2) * block, block, 1), terms[1]], axis=1
    ).astype(jnp.bfloat16)
    own = jnp.concatenate(
        [lax.dynamic_slice_in_dim(terms[0], layer_index * block, block, 1), terms[1]], axis=1
    )
    incoming = lax.ppermute(outgoing, "layer", [(i, i ^ 2) for i in range(layers)])
    features = ((own + incoming.astype(jnp.float32)) / seq_len).astype(jnp.bfloat16)
    train_block = jnp.transpose(features[:, :block].reshape(ckpts, 2, half, ins), (1, 2, 0, 3))
    train_message = jnp.broadcast_to(train_block, (cols_b, pairs, 2, half, ckpts, ins))
    train_message = train_message.reshape(grid, half, ckpts, ins)
    query = features[:, block:].reshape(ckpts, pairs, 2, cols_b, ins)
    query_own = jnp.transpose(query, (3, 1, 2, 0, 4)).reshape(grid, 1, ckpts, ins)
    query_other = jnp.transpose(jnp.flip(query, 2), (3, 1, 2, 0, 4)).reshape(grid, 1, ckpts, ins)
    message = jnp.concatenate([train_message, query_own, query_other], axis=1)
    message, hessian_other = lax.optimization_barrier((message, hessian_other))
    received = lax.all_to_all(message, ("query", "train"), 0, 0)
    train_rows = received[:, :half]
    query_columns = jnp.concatenate([received[:, half], received[:, half + 1]], axis=2)
    partial_pre = jnp.concatenate(
        [
            jnp.einsum("tkci,ckin->ctn", train_rows, part, preferred_element_type=jnp.float32)
            for part in (hessian_own, hessian_other)
        ],
        axis=2,
    )
    scores = jnp.einsum(
        "ctn,qcn->tq",
        partial_pre,
        query_columns.astype(jnp.float32),
        precision=lax.Precision.HIGHEST,
        preferred_element_type=jnp.float32,
    )
    tile_rows = scores.shape[0] // rows_a
    tile_cols = scores.shape[1] // cols_b
    tiles = scores.reshape(cols_b, rows_a, tile_cols, cols_b)
    tiles = jnp.transpose(tiles, (1, 3, 0, 2)).reshape(1, grid, 1, tile_rows * tile_cols)
    tiles = jnp.broadcast_to(tiles, (layers, grid, 1, tile_rows * tile_cols))
    tiles = tiles.reshape(layers * grid, 1, tile_rows * tile_cols)
    shares = lax.all_to_all(tiles, ("layer", "train", "query"), 0, 0)
    return pl.pallas_call(
        add_shares,
        out_shape=jax.ShapeDtypeStruct((tile_rows, tile_cols), jnp.float32),
        compiler_params=pltpu.CompilerParams(vmem_limit_bytes=4 * 1024 * 1024),
        name="add_shares",
    )(shares.reshape(layers * grid, tile_rows * tile_cols))


def solution(mesh):
    tokens = P(None, "layer", ("train", "query"), None, None)
    in_specs = (
        tokens,
        tokens,
        tokens,
        tokens,
        P("layer", None, None),
        P("layer", None, None),
        P(None, "layer", ("train", "query")),
        P(("train", "query")),
        P(("train", "query")),
    )
    return jax.shard_map(
        on_device, mesh=mesh, in_specs=in_specs, out_specs=P("train", "query"), check_vma=False
    )
```

```python
import jax
import jax.numpy as jnp
from jax import lax
from jax.experimental import pallas as pl
from jax.experimental.pallas import tpu as pltpu
from jax.sharding import PartitionSpec as P

CHUNKS = 4
AHEAD = 4


def sketch_kernel(
    train_length,
    query_length,
    train_act,
    train_grad,
    query_act,
    query_grad,
    in_projection,
    out_projection,
    result,
    act,
    grad,
    inner,
    outer,
    arrived,
):
    ckpts, seq_len, width = train_act.shape
    chunk = width // CHUNKS
    rows = 2 * ckpts * seq_len
    copies = []
    for step in range(CHUNKS):
        cols = pl.ds(step * chunk, chunk)
        group = [
            (train_act.at[:, :, cols], act.at[pl.ds(0, ckpts), :, cols]),
            (query_act.at[:, :, cols], act.at[pl.ds(ckpts, ckpts), :, cols]),
            (train_grad.at[:, :, cols], grad.at[pl.ds(0, ckpts), :, cols]),
            (query_grad.at[:, :, cols], grad.at[pl.ds(ckpts, ckpts), :, cols]),
        ]
        group = [
            pltpu.make_async_copy(source, target, arrived.at[step, place])
            for place, (source, target) in enumerate(group)
        ]
        copies.append(group)
    for group in copies[:AHEAD]:
        for copy in group:
            copy.start()
    for step, group in enumerate(copies):
        cols = pl.ds(step * chunk, chunk)
        for copy in group:
            copy.wait()
        for ahead in copies[step + AHEAD : step + AHEAD + 1]:
            for copy in ahead:
                copy.start()
        inner_term = jnp.dot(
            act[:, :, cols].reshape(rows, chunk),
            in_projection[cols],
            preferred_element_type=jnp.float32,
        )
        outer_term = lax.dot_general(
            grad[:, :, cols].reshape(rows, chunk),
            out_projection[:, cols],
            (((1,), (1,)), ((), ())),
            preferred_element_type=jnp.float32,
        )
        if step == 0:
            inner[...] = inner_term
            outer[...] = outer_term
        else:
            inner[...] += inner_term
            outer[...] += outer_term
    for side, length in enumerate((train_length, query_length)):
        for ckpt in range(ckpts):
            part = pl.ds((side * ckpts + ckpt) * seq_len, seq_len)
            kept = outer[part]
            positions = lax.broadcasted_iota(jnp.int32, kept.shape, 0)
            kept = jnp.where(positions < length[0], kept, 0.0).astype(jnp.bfloat16)
            total = lax.dot_general(
                kept,
                inner[part].astype(jnp.bfloat16),
                (((0,), (0,)), ((), ())),
                preferred_element_type=jnp.float32,
            )
            result[side, ckpt] = total


def sketches(train_act, train_grad, query_act, query_grad, in_projection, out_projection, train_length, query_length):
    ckpts, _, _, seq_len, width = train_act.shape
    ins, outs = in_projection.shape[2], out_projection.shape[2]
    flat = [x.reshape(ckpts, seq_len, width) for x in (train_act, train_grad, query_act, query_grad)]
    stay = pl.BlockSpec(memory_space=pl.ANY)
    scalar = pl.BlockSpec(memory_space=pltpu.SMEM)
    held = pl.BlockSpec(memory_space=pltpu.VMEM)
    rows = 2 * ckpts * seq_len
    return pl.pallas_call(
        sketch_kernel,
        out_shape=jax.ShapeDtypeStruct((2, ckpts, outs, ins), jnp.float32),
        in_specs=[scalar, scalar] + [stay] * 4 + [held] * 2,
        out_specs=pl.BlockSpec(memory_space=pltpu.VMEM),
        scratch_shapes=[
            pltpu.VMEM((2 * ckpts, seq_len, width), jnp.bfloat16),
            pltpu.VMEM((2 * ckpts, seq_len, width), jnp.bfloat16),
            pltpu.VMEM((rows, ins), jnp.float32),
            pltpu.VMEM((rows, outs), jnp.float32),
            pltpu.SemaphoreType.DMA((CHUNKS, 4)),
        ],
        compiler_params=pltpu.CompilerParams(vmem_limit_bytes=52 * 1024 * 1024),
        name="sketches",
    )(train_length, query_length, *flat, in_projection[0], out_projection[0].T)


def add_shares(shares, tile):
    total = jnp.sum(shares[...], axis=0, keepdims=True)
    width = tile.shape[1]
    for row in range(tile.shape[0]):
        tile[pl.ds(row, 1)] = total[:, row * width : (row + 1) * width]


def on_device(
    train_act,
    train_grad,
    query_act,
    query_grad,
    in_projection,
    out_projection,
    inverse_hessian,
    train_lengths,
    query_lengths,
):
    seq_len = train_act.shape[3]
    layers = lax.axis_size("layer")
    rows_a, cols_b = lax.axis_size("train"), lax.axis_size("query")
    grid = rows_a * cols_b
    terms = sketches(
        train_act, train_grad, query_act, query_grad, in_projection, out_projection, train_lengths, query_lengths
    )
    _, ckpts, outs, ins = terms.shape
    block = outs // layers
    half = block // 2
    pairs = rows_a // 2
    parity = lax.rem(lax.axis_index("train"), 2)
    hessian = inverse_hessian.reshape(ckpts, 2, half, ins, -1)
    other_half = lax.dynamic_index_in_dim(hessian, 1 - parity, 1, keepdims=False)
    swap = [(i, i ^ 1) for i in range(rows_a)]
    hessian_other = lax.ppermute(other_half, "train", swap)
    hessian_own = lax.dynamic_index_in_dim(hessian, parity, 1, keepdims=False)
    layer_index = lax.axis_index("layer")
    gathered = lax.all_gather(terms, "layer", axis_index_groups=[[i, i + 1] for i in range(0, layers, 2)])
    terms = gathered[0] + gathered[1]
    outgoing = jnp.concatenate(
        [lax.dynamic_slice_in_dim(terms[0], (layer_index ^ 2) * block, block, 1), terms[1]], axis=1
    ).astype(jnp.bfloat16)
    own = jnp.concatenate(
        [lax.dynamic_slice_in_dim(terms[0], layer_index * block, block, 1), terms[1]], axis=1
    )
    incoming = lax.ppermute(outgoing, "layer", [(i, i ^ 2) for i in range(layers)])
    features = ((own + incoming.astype(jnp.float32)) / seq_len).astype(jnp.bfloat16)
    train_block = jnp.transpose(features[:, :block].reshape(ckpts, 2, half, ins), (1, 2, 0, 3))
    query = features[:, block:].reshape(ckpts, pairs, 2, cols_b, ins)
    query_own = jnp.transpose(query, (3, 1, 2, 0, 4))[:, :, :, None]
    query_other = jnp.transpose(jnp.stack([query[:, :, 1], query[:, :, 0]], axis=2), (3, 1, 2, 0, 4))[:, :, :, None]
    row = lax.broadcasted_iota(jnp.int32, (cols_b, pairs, 2, half + 2, ckpts, ins), 3)
    train_rows = jnp.pad(train_block, ((0, 0), (0, 2), (0, 0), (0, 0)))
    message = jnp.where(row < half, train_rows, jnp.where(row == half, query_own, query_other))
    message = message.reshape(grid, half + 2, ckpts, ins)
    message, hessian_other = lax.optimization_barrier((message, hessian_other))
    received = lax.all_to_all(message, ("query", "train"), 0, 0)
    train_rows = received[:, :half]
    query_columns = jnp.concatenate([received[:, half], received[:, half + 1]], axis=2)
    partial_pre = jnp.concatenate(
        [
            jnp.einsum("tkci,ckin->ctn", train_rows, part, preferred_element_type=jnp.float32)
            for part in (hessian_own, hessian_other)
        ],
        axis=2,
    )
    scores = jnp.einsum(
        "ctn,qcn->tq",
        partial_pre,
        query_columns.astype(jnp.float32),
        precision=lax.Precision.HIGHEST,
        preferred_element_type=jnp.float32,
    )
    tile_rows = scores.shape[0] // rows_a
    tile_cols = scores.shape[1] // cols_b
    tiles = scores.reshape(cols_b, rows_a, tile_cols, cols_b)
    tiles = jnp.transpose(tiles, (1, 3, 0, 2)).reshape(1, grid, 1, tile_rows * tile_cols)
    tiles = jnp.broadcast_to(tiles, (layers, grid, 1, tile_rows * tile_cols))
    tiles = tiles.reshape(layers * grid, 1, tile_rows * tile_cols)
    shares = lax.all_to_all(tiles, ("layer", "train", "query"), 0, 0)
    return pl.pallas_call(
        add_shares,
        out_shape=jax.ShapeDtypeStruct((tile_rows, tile_cols), jnp.float32),
        compiler_params=pltpu.CompilerParams(vmem_limit_bytes=4 * 1024 * 1024),
        name="add_shares",
    )(shares.reshape(layers * grid, tile_rows * tile_cols))


def solution(mesh):
    tokens = P(None, "layer", ("train", "query"), None, None)
    in_specs = (
        tokens,
        tokens,
        tokens,
        tokens,
        P("layer", None, None),
        P("layer", None, None),
        P(None, "layer", ("train", "query")),
        P(("train", "query")),
        P(("train", "query")),
    )
    return jax.shard_map(
        on_device, mesh=mesh, in_specs=in_specs, out_specs=P("train", "query"), check_vma=False
    )
```

```python
import jax
import jax.numpy as jnp
from jax import lax
from jax.experimental import pallas as pl
from jax.experimental.pallas import tpu as pltpu
from jax.sharding import PartitionSpec as P

CHUNKS = 4
AHEAD = 4


def sketch_kernel(
    train_length,
    query_length,
    train_act,
    train_grad,
    query_act,
    query_grad,
    in_projection,
    out_projection,
    result,
    act,
    grad,
    inner,
    outer,
    arrived,
):
    ckpts, seq_len, width = train_act.shape
    chunk = width // CHUNKS
    rows = 2 * ckpts * seq_len
    copies = []
    for step in range(CHUNKS):
        cols = pl.ds(step * chunk, chunk)
        group = [
            (train_act.at[:, :, cols], act.at[pl.ds(0, ckpts), :, cols]),
            (query_act.at[:, :, cols], act.at[pl.ds(ckpts, ckpts), :, cols]),
            (train_grad.at[:, :, cols], grad.at[pl.ds(0, ckpts), :, cols]),
            (query_grad.at[:, :, cols], grad.at[pl.ds(ckpts, ckpts), :, cols]),
        ]
        group = [
            pltpu.make_async_copy(source, target, arrived.at[step, place])
            for place, (source, target) in enumerate(group)
        ]
        copies.append(group)
    for group in copies[:AHEAD]:
        for copy in group:
            copy.start()
    for step, group in enumerate(copies):
        cols = pl.ds(step * chunk, chunk)
        for copy in group:
            copy.wait()
        for ahead in copies[step + AHEAD : step + AHEAD + 1]:
            for copy in ahead:
                copy.start()
        inner_term = jnp.dot(
            act[:, :, cols].reshape(rows, chunk),
            in_projection[cols],
            preferred_element_type=jnp.float32,
        )
        outer_term = lax.dot_general(
            grad[:, :, cols].reshape(rows, chunk),
            out_projection[:, cols],
            (((1,), (1,)), ((), ())),
            preferred_element_type=jnp.float32,
        )
        if step == 0:
            inner[...] = inner_term
            outer[...] = outer_term
        else:
            inner[...] += inner_term
            outer[...] += outer_term
    for side, length in enumerate((train_length, query_length)):
        for ckpt in range(ckpts):
            part = pl.ds((side * ckpts + ckpt) * seq_len, seq_len)
            kept = outer[part]
            positions = lax.broadcasted_iota(jnp.int32, kept.shape, 0)
            kept = jnp.where(positions < length[0], kept, 0.0).astype(jnp.bfloat16)
            total = lax.dot_general(
                kept,
                inner[part].astype(jnp.bfloat16),
                (((0,), (0,)), ((), ())),
                preferred_element_type=jnp.float32,
            )
            result[side, ckpt] = total


def sketches(train_act, train_grad, query_act, query_grad, in_projection, out_projection, train_length, query_length):
    ckpts, _, _, seq_len, width = train_act.shape
    ins, outs = in_projection.shape[2], out_projection.shape[2]
    flat = [x.reshape(ckpts, seq_len, width) for x in (train_act, train_grad, query_act, query_grad)]
    stay = pl.BlockSpec(memory_space=pl.ANY)
    scalar = pl.BlockSpec(memory_space=pltpu.SMEM)
    held = pl.BlockSpec(memory_space=pltpu.VMEM)
    rows = 2 * ckpts * seq_len
    return pl.pallas_call(
        sketch_kernel,
        out_shape=jax.ShapeDtypeStruct((2, ckpts, outs, ins), jnp.float32),
        in_specs=[scalar, scalar] + [stay] * 4 + [held] * 2,
        out_specs=pl.BlockSpec(memory_space=pltpu.VMEM),
        scratch_shapes=[
            pltpu.VMEM((2 * ckpts, seq_len, width), jnp.bfloat16),
            pltpu.VMEM((2 * ckpts, seq_len, width), jnp.bfloat16),
            pltpu.VMEM((rows, ins), jnp.float32),
            pltpu.VMEM((rows, outs), jnp.float32),
            pltpu.SemaphoreType.DMA((CHUNKS, 4)),
        ],
        compiler_params=pltpu.CompilerParams(vmem_limit_bytes=52 * 1024 * 1024),
        name="sketches",
    )(train_length, query_length, *flat, in_projection[0], out_projection[0].T)


def add_shares(shares, tile):
    total = jnp.sum(shares[...], axis=0, keepdims=True)
    width = tile.shape[1]
    for row in range(tile.shape[0]):
        tile[pl.ds(row, 1)] = total[:, row * width : (row + 1) * width]


def on_device(
    train_act,
    train_grad,
    query_act,
    query_grad,
    in_projection,
    out_projection,
    inverse_hessian,
    train_lengths,
    query_lengths,
):
    seq_len = train_act.shape[3]
    layers = lax.axis_size("layer")
    rows_a, cols_b = lax.axis_size("train"), lax.axis_size("query")
    grid = rows_a * cols_b
    terms = sketches(
        train_act, train_grad, query_act, query_grad, in_projection, out_projection, train_lengths, query_lengths
    )
    _, ckpts, outs, ins = terms.shape
    block = outs // layers
    half = block // 2
    pairs = rows_a // 2
    parity = lax.rem(lax.axis_index("train"), 2)
    hessian = inverse_hessian.reshape(ckpts, 2, half, ins, -1)
    other_half = lax.dynamic_index_in_dim(hessian, 1 - parity, 1, keepdims=False)
    swap = [(i, i ^ 1) for i in range(rows_a)]
    hessian_other = lax.ppermute(other_half, "train", swap)
    hessian_own = lax.dynamic_index_in_dim(hessian, parity, 1, keepdims=False)
    layer_index = lax.axis_index("layer")
    gathered = lax.all_gather(terms, "layer", axis_index_groups=[[i, i + 1] for i in range(0, layers, 2)])
    terms = gathered[0] + gathered[1]
    outgoing = jnp.concatenate(
        [lax.dynamic_slice_in_dim(terms[0], (layer_index ^ 2) * block, block, 1), terms[1]], axis=1
    ).astype(jnp.bfloat16)
    own = jnp.concatenate(
        [lax.dynamic_slice_in_dim(terms[0], layer_index * block, block, 1), terms[1]], axis=1
    )
    incoming = lax.ppermute(outgoing, "layer", [(i, i ^ 2) for i in range(layers)])
    features = ((own + incoming.astype(jnp.float32)) / seq_len).astype(jnp.bfloat16)
    train_block = jnp.transpose(features[:, :block].reshape(ckpts, 2, half, ins), (1, 2, 0, 3))
    query = features[:, block:].reshape(ckpts, pairs, 2, cols_b, ins)
    query_own = jnp.transpose(query, (3, 1, 2, 0, 4))[:, :, :, None]
    query_other = jnp.transpose(jnp.stack([query[:, :, 1], query[:, :, 0]], axis=2), (3, 1, 2, 0, 4))[:, :, :, None]
    row = lax.broadcasted_iota(jnp.int32, (cols_b, pairs, 2, half + 2, ckpts, ins), 3)
    train_rows = jnp.pad(train_block, ((0, 0), (0, 2), (0, 0), (0, 0)))
    message = jnp.where(row < half, train_rows, jnp.where(row == half, query_own, query_other))
    message = message.reshape(grid, half + 2, ckpts, ins)
    message, hessian_other = lax.optimization_barrier((message, hessian_other))
    received = lax.all_to_all(message, ("query", "train"), 0, 0)
    train_rows = received[:, :half]
    query_columns = jnp.concatenate([received[:, half], received[:, half + 1]], axis=2)
    partial_pre = jnp.concatenate(
        [
            jnp.einsum("tkci,ckin->ctn", train_rows, part, preferred_element_type=jnp.float32)
            for part in (hessian_own, hessian_other)
        ],
        axis=2,
    )
    scores = jnp.einsum(
        "ctn,qcn->tq",
        partial_pre,
        query_columns.astype(jnp.float32),
        precision=lax.Precision.HIGHEST,
        preferred_element_type=jnp.float32,
    )
    tile_rows = scores.shape[0] // rows_a
    tile_cols = scores.shape[1] // cols_b
    tiles = scores.reshape(cols_b, rows_a, tile_cols, cols_b)
    tiles = jnp.transpose(tiles, (3, 1, 0, 2)).reshape(grid, 1, 1, tile_rows * tile_cols)
    tiles = jnp.broadcast_to(tiles, (grid, layers, 1, tile_rows * tile_cols))
    tiles = tiles.reshape(layers * grid, 1, tile_rows * tile_cols)
    shares = lax.all_to_all(tiles, ("query", "train", "layer"), 0, 0)
    return pl.pallas_call(
        add_shares,
        out_shape=jax.ShapeDtypeStruct((tile_rows, tile_cols), jnp.float32),
        compiler_params=pltpu.CompilerParams(vmem_limit_bytes=4 * 1024 * 1024),
        name="add_shares",
    )(shares.reshape(layers * grid, tile_rows * tile_cols))


def solution(mesh):
    tokens = P(None, "layer", ("train", "query"), None, None)
    in_specs = (
        tokens,
        tokens,
        tokens,
        tokens,
        P("layer", None, None),
        P("layer", None, None),
        P(None, "layer", ("train", "query")),
        P(("train", "query")),
        P(("train", "query")),
    )
    return jax.shard_map(
        on_device, mesh=mesh, in_specs=in_specs, out_specs=P("train", "query"), check_vma=False
    )
```
